768 devices in a mesh: section: 16 (over y_lo, x, core), fsdp: 48 (over z, y_hi).
Axes of the slice: x: 4, y: 8 (y_hi: 4, y_lo: 2; y = y_hi * 2 + y_lo), z: 12, core: 2. Of those that a mesh axis runs over, the one named last changes fastest.
Arguments:
- section_input: bfloat16 [16, 256, 12288], P('section', None, 'fsdp'), may hold values from -6 to 6
- stash_held: bfloat16 [16, 256, 12288], P('section', None, 'fsdp'), may hold values from -17 to 17
- upstream: bfloat16 [16, 256, 12288], P('section', None, 'fsdp'), may hold values from -6 to 6
- norm_gain: float32 [16, 12288], P('section', 'fsdp'), may hold values from 0.25 to 1.75
- out_weight: bfloat16 [16, 6144, 12288], P('section', None, 'fsdp'), may hold values from -0.078125 to 0.078125
Outputs:
- section_output: bfloat16 [16, 256, 12288], P('section', None, 'fsdp')
- stash_moved: bfloat16 [16, 256, 12288], P('section', None, 'fsdp')
- input_grad: bfloat16 [16, 256, 12288], P('section', None, 'fsdp')
The draws below stay inside these ranges and needn't reach their ends.
All inputs are finite; a program needn't handle non-finite values.
Results may differ from the reference program's by a relative error of at most 0.012.
The reference program's roundings to bfloat16 on the way (of `fetched`, `normed`, `weights`, `context`, `dcontext` and `dscore`) count: a program that leaves them out, or rounds other values in their place, can miss the bound.
Values may be sent and summed in bfloat16 or wider, within the bound.
A program may use at most 32 MiB of HBM per device.

```python
import math
import jax
import jax.numpy as jnp
from jax import lax

D = 12288
HD = 128
SEQ = 256
SECTIONS = 16


def draw_stash_held(key, part):
    key_base = jax.random.fold_in(key, 11)
    key_rows = jax.random.fold_in(key, 12)
    key_blocks = jax.random.fold_in(key, 13)
    blocks = D // HD
    levels = jnp.exp(jax.random.uniform(key_blocks, (SECTIONS, 1, blocks, 1), jnp.float32, -3.0, 3.0))
    row_scale = jnp.exp(jax.random.uniform(key_rows, (SECTIONS, SEQ, 1, 1), jnp.float32, math.log(0.02), math.log(0.2)))
    base = jax.random.normal(key_base, (SECTIONS, SEQ, blocks, HD), jnp.float32)
    base = jnp.clip(base, -4.0, 4.0)
    values = base * levels * row_scale
    return values.reshape(SECTIONS, SEQ, D).astype(jnp.bfloat16)


def block_scale(own_key, extent, shards, low, top_value):
    factor_of, own = 1.0, jax.random.fold_in(own_key, 6)
    for axis_at, shards_of in shards:
        steps = jnp.exp(jax.random.uniform(jax.random.fold_in(own, axis_at), (shards_of,), jnp.float32, low / len(shards), top_value / len(shards)))
        factor_of = factor_of * jnp.repeat(steps, extent[axis_at] // shards_of).reshape([-1 if axis == axis_at else 1 for axis in range(len(extent))])
    return factor_of


def normal_values(own_key, extent, scale, limit, cuts=(), kind=jnp.bfloat16):
    values = jax.random.normal(own_key, extent, jnp.float32) * scale
    if len(cuts) > 0:
        values = block_scale(own_key, extent, cuts, -0.22, 0.18) * values
    return jnp.clip(values, min=-limit, max=limit).astype(kind)


def setup_inputs(seed: int = 0) -> dict:
    splits = jax.random.split(jax.random.key(seed), 6)
    return {
        "section_input": normal_values(splits[0], (SECTIONS, SEQ, D), 1.0, 6.0, ((0, 16), (2, 48))),
        "stash_held": draw_stash_held(jax.random.fold_in(splits[5], 71), 0),
        "upstream": normal_values(splits[2], (SECTIONS, SEQ, D), 1.0, 6.0, ((0, 16), (2, 48))),
        "norm_gain": jnp.clip(1.0 + 0.15 * jax.random.normal(splits[3], (SECTIONS, D), jnp.float32), 0.25, 1.75),
        "out_weight": normal_values(splits[4], (SECTIONS, D // 2, D), (D // 2) ** -0.5, 0.078125, ((0, 16), (2, 48))),
    }


EPSILON = 1e-05

def attend(normed):
    paired = normed.reshape(SEQ, D // (2 * HD), 2, HD)
    queries = paired[:, :, 0].astype(jnp.float32)
    keyvals = paired[:, :, 1].astype(jnp.float32)
    shrink = HD ** (-0.5)
    scores = jnp.einsum('qhd,khd->hqk', queries, keyvals) * shrink
    allowed = jnp.arange(SEQ)[:, None] >= jnp.arange(SEQ)[None, :]
    scores = jnp.where(allowed[None], scores, -1e+30)
    probs = jax.nn.softmax(scores, axis=-1)
    weights = probs.astype(jnp.bfloat16)
    context = jnp.einsum('hqk,khd->qhd', weights.astype(jnp.float32), keyvals)
    context = context.astype(jnp.bfloat16).reshape(SEQ, -1)
    return (queries, keyvals, probs, weights, context)

def normalize(values, gain_row):
    inverse = lax.rsqrt(lax.optimization_barrier(jnp.sum(values * values, axis=-1)) / D + EPSILON)
    normed = (values * inverse[:, None] * gain_row[None]).astype(jnp.bfloat16)
    return (inverse, normed)

def one_section(items):
    fresh, fetched, grad_rows, gain_row, weight = items
    fresh_f = fresh.astype(jnp.float32)
    inverse_f, normed_f = normalize(fresh_f, gain_row)
    context_f = attend(normed_f)[4]
    output = (fresh_f + jnp.dot(context_f, weight, preferred_element_type=jnp.float32)).astype(jnp.bfloat16)
    held_f = fetched.astype(jnp.float32)
    inverse_b, normed_b = normalize(held_f, gain_row)
    queries, keyvals, probs, weights, unused = attend(normed_b)
    dcontext = jnp.dot(grad_rows, weight.T, preferred_element_type=jnp.float32).astype(jnp.bfloat16)
    dcontext = dcontext.reshape(SEQ, D // (2 * HD), HD).astype(jnp.float32)
    dprob = jnp.einsum('qhd,khd->hqk', dcontext, keyvals)
    dvalue = jnp.einsum('hqk,qhd->khd', weights.astype(jnp.float32), dcontext)
    shrink = HD ** (-0.5)
    dscore = (probs * (dprob - lax.optimization_barrier(jnp.sum(dprob * probs, axis=-1, keepdims=True))) * shrink).astype(jnp.bfloat16)
    dscore = dscore.astype(jnp.float32)
    dquery = jnp.einsum('hqk,khd->qhd', dscore, keyvals)
    dkey = jnp.einsum('hqk,qhd->khd', dscore, queries)
    dnormed = jnp.stack([dquery, dvalue + dkey], axis=2).reshape(SEQ, D)
    scaled = dnormed * gain_row[None]
    moment = lax.optimization_barrier(jnp.sum(scaled * held_f, axis=-1))
    grad_in = grad_rows.astype(jnp.float32) + inverse_b[:, None] * scaled
    grad_in = grad_in - held_f * (inverse_b ** 3 * moment / D)[:, None]
    return (output, grad_in.astype(jnp.bfloat16))

def reference(section_input, stash_held, upstream, norm_gain, out_weight):
    fetched_all = stash_held[::-1]
    section_output, input_grad = lax.map(one_section, (section_input, fetched_all, upstream, norm_gain, out_weight))
    stash_moved = section_input[::-1]
    return (section_output, stash_moved, input_grad)
```

```python
import functools

import jax
import jax.numpy as jnp
from jax import lax
from jax.experimental import pallas as pl
from jax.experimental.pallas import tpu as pltpu
from jax.sharding import PartitionSpec as P

HD = 128
EPSILON = 1e-05
F32 = jnp.float32
BF16 = jnp.bfloat16
YS = 4


def dot(a, b):
    return lax.dot_general(a, b, (((1,), (0,)), ((), ())), preferred_element_type=F32)


def dot_t(a, b):
    return lax.dot_general(a, b, (((1,), (1,)), ((), ())), preferred_element_type=F32)


def columns(tile, row):
    halves = [
        jnp.transpose(jnp.broadcast_to(tile[row + i : row + i + 1], (HD, HD))) for i in range(2)
    ]
    half = jnp.concatenate(halves, axis=0)
    return jnp.concatenate([half, half], axis=1)


def token_sums(values):
    return jnp.sum(jnp.transpose(values), axis=0, keepdims=True)


def causal_probs(normed):
    queries, keyvals = normed[:, :HD], normed[:, HD:]
    scores = dot_t(queries, keyvals) * (HD**-0.5)
    rows = lax.broadcasted_iota(jnp.int32, scores.shape, 0)
    cols = lax.broadcasted_iota(jnp.int32, scores.shape, 1)
    scores = jnp.where(rows >= cols, scores, -1e30)
    shifted = jnp.exp(scores - jnp.max(scores, axis=-1, keepdims=True))
    return shifted / jnp.sum(shifted, axis=-1, keepdims=True)


def body(
    sections, zs, ys, fresh_hbm, held_hbm, up_hbm, gain_ref, w_hbm,
    out_ref, moved_ref, gin_ref,
    fresh_v, held_v, up_v, w_v, upt_v, fetched_v, acc_v, own_v, probs_v, normed_v,
    rs_out, rs_in, ys_out, ys_in, ctx_v,
    stat_v, stat_z, stat_y, stat_m, mom_v, mom_z, mom_y,
    load_sem, mir_send, mir_recv, rs_send, rs_recv, ys_send, ys_recv,
    yg_send, yg_recv, ag_send, ag_recv,
    sz_send, sz_recv, sy_send, sy_recv, mz_send, mz_recv, my_send, my_recv,
):
    width = zs * ys * 2 * HD
    sec = lax.axis_index("section")
    me = lax.axis_index("fsdp")
    z = me // ys
    y = me % ys
    half = zs // 2

    def at(dz, dy):
        return lax.rem(z + dz + zs, zs) * ys + lax.rem(y + dy + ys, ys)

    def remote(src, dst, send, recv, where):
        return pltpu.make_async_remote_copy(
            src_ref=src, dst_ref=dst, send_sem=send, recv_sem=recv,
            device_id=where, device_id_type=pl.DeviceIdType.MESH,
        )

    mirror = {"section": sections - 1 - sec}
    barrier = pltpu.get_barrier_semaphore()
    peers = [{"fsdp": at(d, 0)} for d in range(1, zs)] + [{"fsdp": at(0, d)} for d in range(1, ys)]
    peers.append(mirror)
    for peer in peers:
        pl.semaphore_signal(barrier, inc=1, device_id=peer, device_id_type=pl.DeviceIdType.MESH)
    loads = [
        pltpu.make_async_copy(src, dst, load_sem.at[i])
        for i, (src, dst) in enumerate(
            ((up_hbm, up_v), (w_hbm, w_v), (fresh_hbm, fresh_v), (held_hbm, held_v))
        )
    ]
    for load in loads:
        load.start()
    loads[0].wait()
    upt_v[...] = jnp.transpose(up_v[...].astype(F32)).astype(BF16)
    loads[1].wait()
    pl.semaphore_wait(barrier, len(peers))

    sent = []

    def partial(dz, j):
        row = at(dz, 1 + j) * HD
        return dot(w_v[pl.ds(pl.multiple_of(row, HD), HD), :], upt_v[...])

    def mine(way, j):
        return (j < ys // 2) == (way == 0)

    def rs_copy(way, k, j):
        return remote(
            rs_out.at[way, k, j], rs_in.at[way, k, j], rs_send.at[way, k, j],
            rs_recv.at[way, k, j], {"fsdp": at(1 - 2 * way, 0)},
        )

    def rs_step(k):
        for j in range(ys):
            for way in range(2):
                if k == 0 and not mine(way, j):
                    continue
                value = partial((1 - 2 * way) * (half - k), j)
                if k > 1 or (k == 1 and mine(way, j)):
                    rs_copy(way, k - 1, j).wait_recv()
                    value = value + rs_in[way, k - 1, j].astype(F32)
                rs_out[way, k, j] = value.astype(BF16)
                copy = rs_copy(way, k, j)
                copy.start()
                sent.append(copy)

    def ys_copy(j):
        return remote(
            ys_out.at[j], ys_in.at[j], ys_send.at[j], ys_recv.at[j], {"fsdp": at(0, 1 + j)}
        )

    def rs_last():
        for j in range(ys):
            value = partial(0, j)
            for way in range(2):
                rs_copy(way, half - 1, j).wait_recv()
                value = value + rs_in[way, half - 1, j].astype(F32)
            if j < ys - 1:
                ys_out[j] = value.astype(BF16)
                copy = ys_copy(j)
                copy.start()
                sent.append(copy)
            else:
                own_v[...] = value

    def z_sum_start(tile, landing, send, recv):
        for d in range(1, zs):
            copy = remote(
                tile, landing.at[d], send.at[d], recv.at[d], {"fsdp": at(d, 0)}
            )
            copy.start()
            sent.append(copy)

    def z_sum_end(tile, landing, send, recv):
        total = tile[...]
        for d in range(1, zs):
            remote(tile, landing.at[d], send.at[d], recv.at[d], {"fsdp": at(d, 0)}).wait_recv()
            total = total + landing[d]
        return total

    def y_sum_start(total, landing, send, recv):
        landing[0] = total
        for d in range(1, ys):
            copy = remote(
                landing.at[0], landing.at[d], send.at[d], recv.at[d], {"fsdp": at(0, d)}
            )
            copy.start()
            sent.append(copy)

    def y_sum_end(landing, send, recv):
        total = landing[0]
        for d in range(1, ys):
            remote(
                landing.at[0], landing.at[d], send.at[d], recv.at[d], {"fsdp": at(0, d)}
            ).wait_recv()
            total = total + landing[d]
        return total

    def yg_copy(d):
        return remote(
            ctx_v.at[me], ctx_v.at[me], yg_send.at[d], yg_recv.at[d], {"fsdp": at(0, d)}
        )

    def yg_wait(d):
        here = ctx_v.at[at(0, -d)]
        remote(here, here, yg_send.at[d], yg_recv.at[d], {"fsdp": at(0, d)}).wait_recv()

    def ag_copy(way, k, j):
        sign = 1 - 2 * way
        block = ctx_v.at[at(-sign * k, -j)]
        return remote(
            block, block, ag_send.at[way, k, j], ag_recv.at[way, k, j], {"fsdp": at(sign, 0)}
        )

    def ag_wait(way, k, j):
        sign = 1 - 2 * way
        block = ctx_v.at[at(-sign * (k + 1), -j)]
        remote(
            block, block, ag_send.at[way, k, j], ag_recv.at[way, k, j], {"fsdp": at(sign, 0)}
        ).wait_recv()

    def project(dz):
        first = lax.rem(z + dz + zs, zs) * ys
        total = acc_v[...]
        for pair in range(ys // 2):
            lhs = jnp.concatenate(
                [ctx_v[first + 2 * pair], ctx_v[first + 2 * pair + 1]], axis=1
            )
            row = (first + 2 * pair) * HD
            total = total + dot(lhs, w_v[pl.ds(pl.multiple_of(row, 2 * HD), 2 * HD), :])
        acc_v[...] = total

    def ag_step(k):
        for j in range(ys):
            for way in range(2):
                if k == 0 and j > 0 and way == 0:
                    yg_wait(j)
                if k > 0:
                    ag_wait(way, k - 1, j)
                if k == half - 1 and not mine(way, j):
                    continue
                copy = ag_copy(way, k, j)
                copy.start()
                sent.append(copy)
        if k == 0:
            project(0)
        else:
            project(-k)
            project(k)

    rs_step(0)
    loads[2].wait()
    loads[3].wait()
    for i, (src, dst) in enumerate(((held_v, fetched_v), (fresh_v, moved_ref))):
        copy = remote(src, dst, mir_send.at[i], mir_recv.at[i], mirror)
        copy.start()
        sent.append(copy)
    fresh = fresh_v[...].astype(F32)
    held = held_v[...].astype(F32)
    fresh_sq = token_sums(fresh * fresh)
    held_sq = token_sums(held * held)
    stat_v[...] = jnp.concatenate(
        [fresh_sq[:, :HD], fresh_sq[:, HD:], held_sq[:, :HD], held_sq[:, HD:],
         jnp.zeros((4, HD), F32)], axis=0
    )
    z_sum_start(stat_v, stat_z, sz_send, sz_recv)
    rs_step(1)
    y_sum_start(z_sum_end(stat_v, stat_z, sz_send, sz_recv), stat_y, sy_send, sy_recv)
    rs_step(2)
    inverse = lax.rsqrt(y_sum_end(stat_y, sy_send, sy_recv) / width + EPSILON)
    stat_m[0] = inverse
    copy = remote(stat_m.at[0], stat_m.at[1], mir_send.at[2], mir_recv.at[2], mirror)
    copy.start()
    sent.append(copy)
    gain = gain_ref[...]
    normed = (fresh_v[...].astype(F32) * columns(inverse, 0) * gain).astype(BF16)
    weights = causal_probs(normed).astype(BF16)
    ctx_v[me] = dot(weights, normed[:, HD:]).astype(BF16)
    for d in range(1, ys):
        copy = yg_copy(d)
        copy.start()
        sent.append(copy)
    acc_v[...] = fresh_v[...].astype(F32)
    rs_step(3)
    ag_step(0)
    for k in range(4, half):
        rs_step(k)
        ag_step(k - 3)
    rs_last()
    remote(held_v, fetched_v, mir_send.at[0], mir_recv.at[0], mirror).wait_recv()
    remote(stat_m.at[0], stat_m.at[1], mir_send.at[2], mir_recv.at[2], mirror).wait_recv()
    inverse_b = columns(stat_m[1], 2)
    normed_b = (fetched_v[...].astype(F32) * inverse_b * gain).astype(BF16)
    normed_v[...] = normed_b
    probs_v[...] = causal_probs(normed_b)
    done = half - 3
    ag_step(done)
    grad_t = own_v[...]
    for j in range(ys - 1):
        ys_copy(j).wait_recv()
        grad_t = grad_t + ys_in[j].astype(F32)
    dcontext = jnp.transpose(grad_t).astype(BF16)
    probs = probs_v[...]
    queries, keyvals = normed_v[:, :HD], normed_v[:, HD:]
    dprob = dot_t(dcontext, keyvals)
    dvalue = dot(jnp.transpose(probs).astype(BF16), dcontext)
    dscore = probs * (dprob - jnp.sum(dprob * probs, axis=-1, keepdims=True)) * (HD**-0.5)
    dquery = dot(dscore.astype(BF16), keyvals)
    dkey = dot(jnp.transpose(dscore).astype(BF16), queries)
    scaled = jnp.concatenate([dquery, dvalue + dkey], axis=1) * gain
    probs_v[...] = scaled
    moment = token_sums(scaled * fetched_v[...].astype(F32))
    mom_v[...] = jnp.concatenate(
        [moment[:, :HD], moment[:, HD:], jnp.zeros((6, HD), F32)], axis=0
    )
    z_sum_start(mom_v, mom_z, mz_send, mz_recv)
    ag_step(done + 1)
    y_sum_start(z_sum_end(mom_v, mom_z, mz_send, mz_recv), mom_y, my_send, my_recv)
    ag_step(done + 2)
    total = columns(y_sum_end(mom_y, my_send, my_recv), 0)
    inverse_b = columns(stat_m[1], 2)
    grad_in = up_v[...].astype(F32) + inverse_b * probs_v[...]
    grad_in = grad_in - fetched_v[...].astype(F32) * (
        inverse_b * inverse_b * inverse_b * total / width
    )
    gin_ref[...] = grad_in.astype(BF16)
    for j in range(ys):
        ag_wait(0 if mine(0, j) else 1, half - 1, j)
    project(half)
    out_ref[...] = acc_v[...].astype(BF16)
    remote(fresh_v, moved_ref, mir_send.at[1], mir_recv.at[1], mirror).wait_recv()
    for copy in sent:
        copy.wait_send()


def local(ys, sections, section_input, stash_held, upstream, norm_gain, out_weight):
    tokens, part = section_input.shape[1:]
    heads = out_weight.shape[1] // HD
    zs = heads // ys
    half = zs // 2
    dma = pltpu.SemaphoreType.DMA
    square = (tokens, part)
    whole = pl.BlockSpec(memory_space=pltpu.VMEM)
    anywhere = pl.BlockSpec(memory_space=pl.ANY)
    scratch = [
        pltpu.VMEM(square, BF16),
        pltpu.VMEM(square, BF16),
        pltpu.VMEM(square, BF16),
        pltpu.VMEM((heads * HD, part), BF16),
        pltpu.VMEM((part, tokens), BF16),
        pltpu.VMEM(square, BF16),
        pltpu.VMEM(square, F32),
        pltpu.VMEM((HD, tokens), F32),
        pltpu.VMEM((tokens, tokens), F32),
        pltpu.VMEM(square, BF16),
        pltpu.VMEM((2, half, ys, HD, tokens), BF16),
        pltpu.VMEM((2, half, ys, HD, tokens), BF16),
        pltpu.VMEM((ys, HD, tokens), BF16),
        pltpu.VMEM((ys, HD, tokens), BF16),
        pltpu.VMEM((heads, tokens, HD), BF16),
        pltpu.VMEM((8, HD), F32),
        pltpu.VMEM((zs, 8, HD), F32),
        pltpu.VMEM((ys, 8, HD), F32),
        pltpu.VMEM((2, 8, HD), F32),
        pltpu.VMEM((8, HD), F32),
        pltpu.VMEM((zs, 8, HD), F32),
        pltpu.VMEM((ys, 8, HD), F32),
        dma((4,)), dma((3,)), dma((3,)),
        dma((2, half, ys)), dma((2, half, ys)), dma((ys,)), dma((ys,)),
        dma((ys,)), dma((ys,)), dma((2, half, ys)), dma((2, half, ys)),
        dma((zs,)), dma((zs,)), dma((ys,)), dma((ys,)),
        dma((zs,)), dma((zs,)), dma((ys,)), dma((ys,)),
    ]
    result = jax.ShapeDtypeStruct(square, BF16)
    output, moved, grad_in = pl.pallas_call(
        functools.partial(body, sections, zs, ys),
        out_shape=(result, result, result),
        in_specs=[anywhere, anywhere, anywhere, whole, anywhere],
        out_specs=(whole, anywhere, whole),
        scratch_shapes=scratch,
        compiler_params=pltpu.CompilerParams(
            collective_id=0, has_side_effects=True, vmem_limit_bytes=48 * 1024 * 1024
        ),
        name="relay_tick",
    )(section_input[0], stash_held[0], upstream[0], norm_gain, out_weight[0])
    return output[None], moved[None], grad_in[None]


def solution(mesh):
    wide = P("section", None, "fsdp")
    return jax.shard_map(
        functools.partial(local, YS, mesh.shape["section"]),
        mesh=mesh,
        in_specs=(wide, wide, wide, P("section", "fsdp"), wide),
        out_specs=(wide, wide, wide),
        check_vma=False,
    )
```

```python
import functools

import jax
import jax.numpy as jnp
from jax import lax
from jax.experimental import pallas as pl
from jax.experimental.pallas import tpu as pltpu
from jax.sharding import PartitionSpec as P

HD = 128
EPSILON = 1e-05
F32 = jnp.float32
BF16 = jnp.bfloat16
YS = 4
SUM_FIRST = 80
GATHER_FIRST = 176


def dot(a, b):
    return lax.dot_general(a, b, (((1,), (0,)), ((), ())), preferred_element_type=F32)


def dot_t(a, b):
    return lax.dot_general(a, b, (((1,), (1,)), ((), ())), preferred_element_type=F32)


def columns(tile, row):
    halves = [
        jnp.transpose(jnp.broadcast_to(tile[row + i : row + i + 1], (HD, HD))) for i in range(2)
    ]
    half = jnp.concatenate(halves, axis=0)
    return jnp.concatenate([half, half], axis=1)


def token_sums(values):
    return jnp.sum(jnp.transpose(values), axis=0, keepdims=True)


def causal_probs(normed):
    queries, keyvals = normed[:, :HD], normed[:, HD:]
    scores = dot_t(queries, keyvals) * (HD**-0.5)
    rows = lax.broadcasted_iota(jnp.int32, scores.shape, 0)
    cols = lax.broadcasted_iota(jnp.int32, scores.shape, 1)
    scores = jnp.where(rows >= cols, scores, -1e30)
    shifted = jnp.exp(scores - jnp.max(scores, axis=-1, keepdims=True))
    return shifted / jnp.sum(shifted, axis=-1, keepdims=True)


def body(
    sections, zs, ys, fresh_hbm, held_hbm, up_hbm, gain_hbm, w_hbm,
    out_ref, moved_ref, gin_ref,
    fresh_v, held_v, up_v, gain_v, w_v, upt_v, fetched_v, acc_v, own_v, probs_v, normed_v,
    a_out, a_in, ay_out, ay_in, b0_out, b0_in, b1_out, b1_in, bz_out, bz_in, ctx_v,
    stat_v, stat_z, stat_y, stat_m, mom_v, mom_z, mom_y,
    load_sem, mir_send, mir_recv, a_send, a_recv, ay_send, ay_recv,
    b0_send, b0_recv, b1_send, b1_recv, bz_send, bz_recv,
    gy_send, gy_recv, ga_send, ga_recv, gz_send, gz_recv, h0_send, h0_recv, h1_send, h1_recv,
    sz_send, sz_recv, sy_send, sy_recv, mz_send, mz_recv, my_send, my_recv,
):
    width = zs * ys * 2 * HD
    tokens = fresh_v.shape[0]
    half = zs // 2
    fa, fb = SUM_FIRST, HD - SUM_FIRST
    ta, tb = GATHER_FIRST, tokens - GATHER_FIRST
    sec = lax.axis_index("section")
    me = lax.axis_index("fsdp")
    z = me // ys
    y = me % ys
    signs = (1, -1)

    def at(dz, dy):
        return lax.rem(z + dz + zs, zs) * ys + lax.rem(y + dy + ys, ys)

    def remote(src, dst, send, recv, where):
        return pltpu.make_async_remote_copy(
            src_ref=src, dst_ref=dst, send_sem=send, recv_sem=recv,
            device_id=where, device_id_type=pl.DeviceIdType.MESH,
        )

    mirror = {"section": sections - 1 - sec}
    barrier = pltpu.get_barrier_semaphore()
    peers = [{"fsdp": at(d, 0)} for d in range(1, zs)] + [{"fsdp": at(0, d)} for d in range(1, ys)]
    peers.append(mirror)
    quarter = w_v.shape[0] // 4
    pieces = [(w_hbm.at[pl.ds(i * quarter, quarter)], w_v.at[pl.ds(i * quarter, quarter)]) for i in range(4)]
    loads = [
        pltpu.make_async_copy(src, dst, load_sem.at[i])
        for i, (src, dst) in enumerate(
            [(fresh_hbm, fresh_v), (held_hbm, held_v), (up_hbm, up_v), *pieces, (gain_hbm, gain_v)]
        )
    ]
    for load in loads:
        load.start()
    for peer in peers:
        pl.semaphore_signal(barrier, inc=1, device_id=peer, device_id_type=pl.DeviceIdType.MESH)

    sent = []

    def start(copy):
        copy.start()
        sent.append(copy)

    def drain():
        for copy in sent:
            copy.wait_send()
        sent.clear()

    def partial(dz, dy, low, count):
        row = pl.multiple_of(at(dz, dy) * HD + low, 16)
        return dot(w_v[pl.ds(row, count), :], upt_v[...])

    def mine(way, j):
        return (j < ys // 2) == (way == 0)

    def a_copy(way, k, j):
        return remote(
            a_out.at[way, k, j], a_in.at[way, k, j], a_send.at[way, k, j], a_recv.at[way, k, j],
            {"fsdp": at(signs[way], 0)},
        )

    def a_step(k, j):
        for way in range(2):
            if k == 0 and not mine(way, j):
                continue
            value = partial(signs[way] * (half - k), 1 + j, 0, fa)
            if k > 1 or (k == 1 and mine(way, j)):
                a_copy(way, k - 1, j).wait_recv()
                value = value + a_in[way, k - 1, j].astype(F32)
            a_out[way, k, j] = value.astype(BF16)
            if k > 0:
                start(a_copy(way, k, j))

    def ay_copy(j):
        return remote(
            ay_out.at[j], ay_in.at[j], ay_send.at[j], ay_recv.at[j], {"fsdp": at(0, 1 + j)}
        )

    def a_last(j):
        value = partial(0, 1 + j, 0, fa)
        for way in range(2):
            a_copy(way, half - 1, j).wait_recv()
            value = value + a_in[way, half - 1, j].astype(F32)
        if j < ys - 1:
            ay_out[j] = value.astype(BF16)
            start(ay_copy(j))
        else:
            own_v[:fa] = value

    def of_way(d):
        return 0 if d > 0 else 1

    def b0_copy(d):
        i = d % zs
        return remote(
            b0_out.at[i], b0_in.at[i], b0_send.at[i], b0_recv.at[i],
            {"fsdp": at(0, signs[of_way(d)])},
        )

    def b1_copy(way, d):
        i = d % zs
        return remote(
            b1_out.at[way, i], b1_in.at[way, i], b1_send.at[way, i], b1_recv.at[way, i],
            {"fsdp": at(0, signs[way])},
        )

    def b1_step(d):
        for way in range(2):
            value = partial(d, signs[way], fa, fb)
            if of_way(d) == way:
                b0_copy(d).wait_recv()
                value = value + b0_in[d % zs].astype(F32)
            b1_out[way, d % zs] = value.astype(BF16)
            start(b1_copy(way, d))

    def y_total(d):
        value = partial(d, 0, fa, fb)
        for way in range(2):
            b1_copy(way, d).wait_recv()
            value = value + b1_in[way, d % zs].astype(F32)
        return value

    def bz_copy(way, k):
        return remote(
            bz_out.at[way, k], bz_in.at[way, k], bz_send.at[way, k], bz_recv.at[way, k],
            {"fsdp": at(signs[way], 0)},
        )

    def bz_step(k):
        for way in range(2):
            if k < way:
                continue
            value = y_total(signs[way] * (half - k))
            if k > way:
                bz_copy(way, k - 1).wait_recv()
                value = value + bz_in[way, k - 1].astype(F32)
            bz_out[way, k] = value.astype(BF16)
            start(bz_copy(way, k))

    def bz_last():
        value = y_total(0)
        for way in range(2):
            if half - 1 >= way:
                bz_copy(way, half - 1).wait_recv()
                value = value + bz_in[way, half - 1].astype(F32)
        own_v[fa:] = value

    def z_sum_start(tile, landing, send, recv):
        for d in range(1, zs):
            start(remote(tile, landing.at[d], send.at[d], recv.at[d], {"fsdp": at(d, 0)}))

    def z_sum_end(tile, landing, send, recv):
        total = tile[...]
        for d in range(1, zs):
            remote(tile, landing.at[d], send.at[d], recv.at[d], {"fsdp": at(d, 0)}).wait_recv()
            total = total + landing[d]
        return total

    def y_sum_start(total, landing, send, recv):
        landing[0] = total
        for d in range(1, ys):
            start(
                remote(landing.at[0], landing.at[d], send.at[d], recv.at[d], {"fsdp": at(0, d)})
            )

    def y_sum_end(landing, send, recv):
        total = landing[0]
        for d in range(1, ys):
            remote(
                landing.at[0], landing.at[d], send.at[d], recv.at[d], {"fsdp": at(0, d)}
            ).wait_recv()
            total = total + landing[d]
        return total

    def first(dz, dy):
        return ctx_v.at[at(dz, dy), pl.ds(0, ta)]

    def second(dz, dy):
        return ctx_v.at[at(dz, dy), pl.ds(ta, tb)]

    def gy_copy(d, block):
        return remote(block, block, gy_send.at[d], gy_recv.at[d], {"fsdp": at(0, d)})

    def ga_copy(way, k, j, block):
        return remote(
            block, block, ga_send.at[way, k, j], ga_recv.at[way, k, j], {"fsdp": at(signs[way], 0)}
        )

    def ga_step(k, j):
        if k == 0 and j > 0:
            gy_copy(j, first(0, -j)).wait_recv()
        for way in range(2):
            block = first(-signs[way] * k, -j)
            if k > 0:
                ga_copy(way, k - 1, j, block).wait_recv()
            if k < half - 1 or mine(way, j):
                start(ga_copy(way, k, j, block))

    def gz_copy(way, k, block):
        return remote(
            block, block, gz_send.at[way, k], gz_recv.at[way, k], {"fsdp": at(signs[way], 0)}
        )

    def h0_copy(way, d, block):
        i = d % zs
        return remote(
            block, block, h0_send.at[way, i], h0_recv.at[way, i], {"fsdp": at(0, signs[way])}
        )

    def h1_copy(d, block):
        i = d % zs
        return remote(
            block, block, h1_send.at[i], h1_recv.at[i], {"fsdp": at(0, signs[of_way(d)])}
        )

    def gz_step(s):
        for way in range(2):
            d = -signs[way] * s
            if (s == half and way == 0) or (s == 0 and way == 1):
                continue
            block = second(d, 0)
            if s > 0:
                gz_copy(way, s - 1, block).wait_recv()
            for to in range(2) if s == 0 else (way,):
                if s < half - 1 + to:
                    start(gz_copy(to, s, block))

    def h0_step(s):
        for d in both(s):
            for way in range(2):
                start(h0_copy(way, d, second(d, 0)))

    def both(s):
        return (s,) if s in (0, half) else (s, -s)

    def h1_step(s):
        for d in both(s):
            for way in range(2):
                block = second(d, -signs[way])
                h0_copy(way, d, block).wait_recv()
                if way == of_way(d):
                    start(h1_copy(d, block))

    def h1_end(s):
        for d in both(s):
            h1_copy(d, second(d, 2)).wait_recv()
            project(d, ta, tb)

    def project(dz, low, count):
        head = lax.rem(z + dz + zs, zs) * ys
        total = acc_v[low : low + count]
        for pair in range(ys // 2):
            lhs = jnp.concatenate(
                [ctx_v[head + 2 * pair + i, low : low + count] for i in range(2)], axis=1
            )
            row = pl.multiple_of((head + 2 * pair) * HD, 2 * HD)
            total = total + dot(lhs, w_v[pl.ds(row, 2 * HD), :])
        acc_v[low : low + count] = total

    def ga_slot(s, fresh_from=0):
        if s < half:
            for j in range(fresh_from, ys):
                ga_step(s, j)
        else:
            for j in range(ys):
                way = 0 if mine(0, j) else 1
                ga_copy(way, half - 1, j, first(half, -j)).wait_recv()
        for d in both(s):
            project(d, 0, ta)

    loads[0].wait()
    fresh = fresh_v[...].astype(F32)
    fresh_sq = token_sums(fresh * fresh)
    loads[1].wait()
    held = held_v[...].astype(F32)
    held_sq = token_sums(held * held)
    stats = jnp.concatenate(
        [fresh_sq[:, :HD], fresh_sq[:, HD:], held_sq[:, :HD], held_sq[:, HD:],
         jnp.zeros((4, HD), F32)], axis=0
    )
    loads[2].wait()
    upt_v[...] = jnp.transpose(up_v[...].astype(F32)).astype(BF16)
    pl.semaphore_wait(barrier, len(peers))
    y_sum_start(stats, stat_y, sy_send, sy_recv)
    for load in loads[3:]:
        load.wait()
    gain = gain_v[...]
    farthest = [half]
    for k in range(half - 1, 0, -1):
        farthest += [k, -k]
    farthest.append(0)
    for j in range(ys):
        a_step(0, j)
        start(a_copy(0 if mine(0, j) else 1, 0, j))
    for d in farthest:
        b0_out[d % zs] = partial(d, 2, fa, fb).astype(BF16)
        start(b0_copy(d))

    def stats_middle():
        stat_v[...] = y_sum_end(stat_y, sy_send, sy_recv)
        z_sum_start(stat_v, stat_z, sz_send, sz_recv)

    def mirror_start(i):
        src, dst = ((held_v, fetched_v), (fresh_v, moved_ref))[i]
        start(remote(src, dst, mir_send.at[i], mir_recv.at[i], mirror))

    def forward_attention():
        inverse = lax.rsqrt(z_sum_end(stat_v, stat_z, sz_send, sz_recv) / width + EPSILON)
        stat_m[0] = inverse
        start(remote(stat_m.at[0], stat_m.at[1], mir_send.at[2], mir_recv.at[2], mirror))
        values = fresh_v[...].astype(F32)
        normed = (values * columns(inverse, 0) * gain).astype(BF16)
        weights = causal_probs(normed).astype(BF16)
        ctx_v[me] = dot(weights, normed[:, HD:]).astype(BF16)
        acc_v[...] = values

    def backward_probs():
        remote(held_v, fetched_v, mir_send.at[0], mir_recv.at[0], mirror).wait_recv()
        remote(stat_m.at[0], stat_m.at[1], mir_send.at[2], mir_recv.at[2], mirror).wait_recv()
        normed_v[...] = (fetched_v[...].astype(F32) * columns(stat_m[1], 2) * gain).astype(BF16)
        probs_v[...] = causal_probs(normed_v[...])

    def backward_attention():
        grad_t = own_v[:fa]
        for j in range(ys - 1):
            ay_copy(j).wait_recv()
            grad_t = grad_t + ay_in[j].astype(F32)
        own_v[:fa] = grad_t
        dcontext = jnp.transpose(own_v[...]).astype(BF16)
        probs = probs_v[...]
        queries, keyvals = normed_v[:, :HD], normed_v[:, HD:]
        dprob = dot_t(dcontext, keyvals)
        dvalue = dot(jnp.transpose(probs).astype(BF16), dcontext)
        dscore = probs * (dprob - jnp.sum(dprob * probs, axis=-1, keepdims=True)) * (HD**-0.5)
        dquery = dot(dscore.astype(BF16), keyvals)
        dkey = dot(jnp.transpose(dscore).astype(BF16), queries)
        scaled = jnp.concatenate([dquery, dvalue + dkey], axis=1) * gain
        probs_v[...] = scaled
        moment = token_sums(scaled * fetched_v[...].astype(F32))
        mom_v[...] = jnp.concatenate(
            [moment[:, :HD], moment[:, HD:], jnp.zeros((6, HD), F32)], axis=0
        )
        z_sum_start(mom_v, mom_z, mz_send, mz_recv)

    def moment_middle():
        y_sum_start(z_sum_end(mom_v, mom_z, mz_send, mz_recv), mom_y, my_send, my_recv)

    def backward_end():
        total = columns(y_sum_end(mom_y, my_send, my_recv), 0)
        inverse = columns(stat_m[1], 2)
        grad_in = up_v[...].astype(F32) + inverse * probs_v[...]
        grad_in = grad_in - fetched_v[...].astype(F32) * (inverse**3 * total / width)
        gin_ref[...] = grad_in.astype(BF16)

    def gy_start():
        for d in range(1, ys):
            start(gy_copy(d, first(0, 0)))

    beside = {(k, j): [] for k in range(1, half) for j in range(ys)}

    def add(slot, step, what, *of):
        at_step = (slot, step) if slot < half else (half - 1, ys - 1)
        beside[at_step].append(functools.partial(what, *of))

    for i, d in enumerate(farthest[:3]):
        add(1, i + 1, b1_step, d)
    add(1, 3, stats_middle)
    for i, d in enumerate(farthest[3:7]):
        add(2, i, b1_step, d)
    add(2, 3, mirror_start, 0)
    for d in farthest[7:]:
        add(2, 3, b1_step, d)
    add(3, 0, forward_attention)
    add(3, 0, gz_step, 0)
    add(3, 2, gy_start)
    add(3, 3, ga_step, 0, 0)
    places = ((3, 3), (4, 1), (4, 3), (5, 1), (5, 3))
    for k in range(half - 1):
        add(*places[k], bz_step, k)
        add(*places[k], gz_step, k + 1)
    if half < 3:
        add(3, 3, gz_step, 2)
    for k in range(1, half):
        for j in range(ys):
            a_step(k, j)
            for what in beside[k, j]:
                what()
    for j in range(ys):
        a_last(j)
    h0_step(0)
    bz_step(half - 1)
    if half > 2:
        gz_step(half)
    bz_last()
    backward_probs()
    h0_step(1)
    ga_slot(0, 1)
    backward_attention()
    h0_turn = iter(range(2, half + 1))
    h1_turn = iter(range(half + 1))
    h1_begun = 0
    h1_done = 0
    for s in range(1, half):
        for count in range(2 if s == 2 else 1):
            h0_next = next(h0_turn, None)
            if h0_next is not None:
                h0_step(h0_next)
        ga_slot(s)
        if s == 1:
            mirror_start(1)
        for count in range(2 if s in (1, 3) else 1):
            h1_step(next(h1_turn))
            h1_begun += 1
        while h1_done < h1_begun - 2:
            h1_end(h1_done)
            h1_done += 1
        if s == min(2, half - 1):
            moment_middle()
        if s == min(4, half - 1):
            backward_end()
    for s in h0_turn:
        h0_step(s)
    drain()
    ga_slot(half)
    for s in h1_turn:
        h1_step(s)
    for s in range(h1_done, half + 1):
        h1_end(s)
    out_ref[...] = acc_v[...].astype(BF16)
    remote(fresh_v, moved_ref, mir_send.at[1], mir_recv.at[1], mirror).wait_recv()
    drain()


def local(ys, sections, section_input, stash_held, upstream, norm_gain, out_weight):
    tokens, part = section_input.shape[1:]
    heads = out_weight.shape[1] // HD
    zs = heads // ys
    half = zs // 2
    fb = HD - SUM_FIRST
    dma = pltpu.SemaphoreType.DMA
    square = (tokens, part)
    whole = pl.BlockSpec(memory_space=pltpu.VMEM)
    anywhere = pl.BlockSpec(memory_space=pl.ANY)
    buffers = [
        (square, BF16),
        (square, BF16),
        (square, BF16),
        ((1, part), F32),
        ((heads * HD, part), BF16),
        ((part, tokens), BF16),
        (square, BF16),
        (square, F32),
        ((HD, tokens), F32),
        ((tokens, tokens), F32),
        (square, BF16),
        ((2, half, ys, SUM_FIRST, tokens), BF16),
        ((2, half, ys, SUM_FIRST, tokens), BF16),
        ((ys, SUM_FIRST, tokens), BF16),
        ((ys, SUM_FIRST, tokens), BF16),
        ((zs, fb, tokens), BF16),
        ((zs, fb, tokens), BF16),
        ((2, zs, fb, tokens), BF16),
        ((2, zs, fb, tokens), BF16),
        ((2, half, fb, tokens), BF16),
        ((2, half, fb, tokens), BF16),
        ((heads, tokens, HD), BF16),
        ((8, HD), F32),
        ((zs, 8, HD), F32),
        ((ys, 8, HD), F32),
        ((2, 8, HD), F32),
        ((8, HD), F32),
        ((zs, 8, HD), F32),
        ((ys, 8, HD), F32),
    ]
    semaphores = [
        (8,), (3,), (3,), (2, half, ys), (2, half, ys), (ys,), (ys,),
        (zs,), (zs,), (2, zs), (2, zs), (2, half), (2, half),
        (ys,), (ys,), (2, half, ys), (2, half, ys), (2, half), (2, half),
        (2, zs), (2, zs), (zs,), (zs,),
        (zs,), (zs,), (ys,), (ys,), (zs,), (zs,), (ys,), (ys,),
    ]
    result = jax.ShapeDtypeStruct(square, BF16)
    output, moved, grad_in = pl.pallas_call(
        functools.partial(body, sections, zs, ys),
        out_shape=(result, result, result),
        in_specs=[pl.BlockSpec(memory_space=pltpu.HBM)] * 5,
        out_specs=(whole, anywhere, whole),
        scratch_shapes=[pltpu.VMEM(*b) for b in buffers] + [dma(s) for s in semaphores],
        compiler_params=pltpu.CompilerParams(
            collective_id=0, has_side_effects=True, vmem_limit_bytes=60 * 1024 * 1024
        ),
        name="relay_tick",
    )(section_input[0], stash_held[0], upstream[0], norm_gain, out_weight[0])
    return output[None], moved[None], grad_in[None]


def solution(mesh):
    wide = P("section", None, "fsdp")
    return jax.shard_map(
        functools.partial(local, YS, mesh.shape["section"]),
        mesh=mesh,
        in_specs=(wide, wide, wide, P("section", "fsdp"), wide),
        out_specs=(wide, wide, wide),
        check_vma=False,
    )
```

```python
import functools

import jax
import jax.numpy as jnp
from jax import lax
from jax.experimental import pallas as pl
from jax.experimental.pallas import tpu as pltpu
from jax.sharding import PartitionSpec as P

HD = 128
EPSILON = 1e-05
F32 = jnp.float32
BF16 = jnp.bfloat16
YS = 4
SUM_FIRST = 96
GATHER_FIRST = 192


def dot(a, b):
    return lax.dot_general(a, b, (((1,), (0,)), ((), ())), preferred_element_type=F32)


def dot_t(a, b):
    return lax.dot_general(a, b, (((1,), (1,)), ((), ())), preferred_element_type=F32)


def columns(tile, row):
    halves = [
        jnp.transpose(jnp.broadcast_to(tile[row + i : row + i + 1], (HD, HD))) for i in range(2)
    ]
    half = jnp.concatenate(halves, axis=0)
    return jnp.concatenate([half, half], axis=1)


def token_sums(values):
    return jnp.sum(jnp.transpose(values), axis=0, keepdims=True)


def causal_probs(normed):
    queries, keyvals = normed[:, :HD], normed[:, HD:]
    scores = dot_t(queries, keyvals) * (HD**-0.5)
    rows = lax.broadcasted_iota(jnp.int32, scores.shape, 0)
    cols = lax.broadcasted_iota(jnp.int32, scores.shape, 1)
    scores = jnp.where(rows >= cols, scores, -1e30)
    shifted = jnp.exp(scores - jnp.max(scores, axis=-1, keepdims=True))
    return shifted / jnp.sum(shifted, axis=-1, keepdims=True)


def body(
    sections, zs, ys, fresh_hbm, held_hbm, up_hbm, gain_hbm, w_hbm,
    out_ref, moved_ref, gin_ref,
    fresh_v, held_v, up_v, gain_v, w_v, upt_v, fetched_v, acc_v, own_v, probs_v, normed_v,
    a_out, a_in, ay_out, ay_in, b0_out, b0_in, b1_out, b1_in, bz_out, bz_in, ctx_v,
    stat_v, stat_z, stat_y, stat_m, mom_v, mom_z, mom_y,
    load_sem, mir_send, mir_recv, a_send, a_recv, ay_send, ay_recv,
    b0_send, b0_recv, b1_send, b1_recv, bz_send, bz_recv,
    gy_send, gy_recv, ga_send, ga_recv, gz_send, gz_recv, h0_send, h0_recv, h1_send, h1_recv,
    sz_send, sz_recv, sy_send, sy_recv, mz_send, mz_recv, my_send, my_recv,
):
    width = zs * ys * 2 * HD
    tokens = fresh_v.shape[0]
    half = zs // 2
    fa, fb = SUM_FIRST, HD - SUM_FIRST
    ta, tb = GATHER_FIRST, tokens - GATHER_FIRST
    sec = lax.axis_index("section")
    me = lax.axis_index("fsdp")
    z = me // ys
    y = me % ys
    signs = (1, -1)

    def at(dz, dy):
        return lax.rem(z + dz + zs, zs) * ys + lax.rem(y + dy + ys, ys)

    def remote(src, dst, send, recv, where):
        return pltpu.make_async_remote_copy(
            src_ref=src, dst_ref=dst, send_sem=send, recv_sem=recv,
            device_id=where, device_id_type=pl.DeviceIdType.MESH,
        )

    mirror = {"section": sections - 1 - sec}
    barrier = pltpu.get_barrier_semaphore()
    peers = [{"fsdp": at(d, 0)} for d in range(1, zs)] + [{"fsdp": at(0, d)} for d in range(1, ys)]
    peers.append(mirror)
    quarter = w_v.shape[0] // 4
    pieces = [(w_hbm.at[pl.ds(i * quarter, quarter)], w_v.at[pl.ds(i * quarter, quarter)]) for i in range(4)]
    loads = [
        pltpu.make_async_copy(src, dst, load_sem.at[i])
        for i, (src, dst) in enumerate(
            [(fresh_hbm, fresh_v), (held_hbm, held_v), (up_hbm, up_v), *pieces, (gain_hbm, gain_v)]
        )
    ]
    for load in loads:
        load.start()
    for peer in peers:
        pl.semaphore_signal(barrier, inc=1, device_id=peer, device_id_type=pl.DeviceIdType.MESH)

    sent = []

    def start(copy):
        copy.start()
        sent.append(copy)

    def drain():
        for copy in sent:
            copy.wait_send()
        sent.clear()

    def partial(dz, dy, low, count):
        row = pl.multiple_of(at(dz, dy) * HD + low, 16)
        return dot(w_v[pl.ds(row, count), :], upt_v[...])

    def mine(way, j):
        return (j < ys // 2) == (way == 0)

    def a_copy(way, k, j):
        return remote(
            a_out.at[way, k, j], a_in.at[way, k, j], a_send.at[way, k, j], a_recv.at[way, k, j],
            {"fsdp": at(signs[way], 0)},
        )

    def a_step(k, j):
        for way in range(2):
            if k == 0 and not mine(way, j):
                continue
            value = partial(signs[way] * (half - k), 1 + j, 0, fa)
            if k > 1 or (k == 1 and mine(way, j)):
                a_copy(way, k - 1, j).wait_recv()
                value = value + a_in[way, k - 1, j].astype(F32)
            a_out[way, k, j] = value.astype(BF16)
            if k > 0:
                start(a_copy(way, k, j))

    def ay_copy(j):
        return remote(
            ay_out.at[j], ay_in.at[j], ay_send.at[j], ay_recv.at[j], {"fsdp": at(0, 1 + j)}
        )

    def a_last(j):
        value = partial(0, 1 + j, 0, fa)
        for way in range(2):
            a_copy(way, half - 1, j).wait_recv()
            value = value + a_in[way, half - 1, j].astype(F32)
        if j < ys - 1:
            ay_out[j] = value.astype(BF16)
            start(ay_copy(j))
        else:
            own_v[:fa] = value

    def of_way(d):
        return 0 if d > 0 else 1

    def b0_copy(d):
        i = d % zs
        return remote(
            b0_out.at[i], b0_in.at[i], b0_send.at[i], b0_recv.at[i],
            {"fsdp": at(0, signs[of_way(d)])},
        )

    def b1_copy(way, d):
        i = d % zs
        return remote(
            b1_out.at[way, i], b1_in.at[way, i], b1_send.at[way, i], b1_recv.at[way, i],
            {"fsdp": at(0, signs[way])},
        )

    def b1_step(d):
        for way in range(2):
            value = partial(d, signs[way], fa, fb)
            if of_way(d) == way:
                b0_copy(d).wait_recv()
                value = value + b0_in[d % zs].astype(F32)
            b1_out[way, d % zs] = value.astype(BF16)
            start(b1_copy(way, d))

    def y_total(d):
        value = partial(d, 0, fa, fb)
        for way in range(2):
            b1_copy(way, d).wait_recv()
            value = value + b1_in[way, d % zs].astype(F32)
        return value

    def bz_copy(way, k):
        return remote(
            bz_out.at[way, k], bz_in.at[way, k], bz_send.at[way, k], bz_recv.at[way, k],
            {"fsdp": at(signs[way], 0)},
        )

    def bz_step(k):
        for way in range(2):
            if k < way:
                continue
            value = y_total(signs[way] * (half - k))
            if k > way:
                bz_copy(way, k - 1).wait_recv()
                value = value + bz_in[way, k - 1].astype(F32)
            bz_out[way, k] = value.astype(BF16)
            start(bz_copy(way, k))

    def bz_last():
        value = y_total(0)
        for way in range(2):
            if half - 1 >= way:
                bz_copy(way, half - 1).wait_recv()
                value = value + bz_in[way, half - 1].astype(F32)
        own_v[fa:] = value

    def z_sum_start(tile, landing, send, recv):
        for d in range(1, zs):
            start(remote(tile, landing.at[d], send.at[d], recv.at[d], {"fsdp": at(d, 0)}))

    def z_sum_end(tile, landing, send, recv):
        total = tile[...]
        for d in range(1, zs):
            remote(tile, landing.at[d], send.at[d], recv.at[d], {"fsdp": at(d, 0)}).wait_recv()
            total = total + landing[d]
        return total

    def y_sum_start(total, landing, send, recv):
        landing[0] = total
        for d in range(1, ys):
            start(
                remote(landing.at[0], landing.at[d], send.at[d], recv.at[d], {"fsdp": at(0, d)})
            )

    def y_sum_end(landing, send, recv):
        total = landing[0]
        for d in range(1, ys):
            remote(
                landing.at[0], landing.at[d], send.at[d], recv.at[d], {"fsdp": at(0, d)}
            ).wait_recv()
            total = total + landing[d]
        return total

    def first(dz, dy):
        return ctx_v.at[at(dz, dy), pl.ds(0, ta)]

    def second(dz, dy):
        return ctx_v.at[at(dz, dy), pl.ds(ta, tb)]

    def gy_copy(d, block):
        return remote(block, block, gy_send.at[d], gy_recv.at[d], {"fsdp": at(0, d)})

    def ga_copy(way, k, j, block):
        return remote(
            block, block, ga_send.at[way, k, j], ga_recv.at[way, k, j], {"fsdp": at(signs[way], 0)}
        )

    def ga_step(k, j):
        if k == 0 and j > 0:
            gy_copy(j, first(0, -j)).wait_recv()
        for way in range(2):
            block = first(-signs[way] * k, -j)
            if k > 0:
                ga_copy(way, k - 1, j, block).wait_recv()
            if k < half - 1 or mine(way, j):
                start(ga_copy(way, k, j, block))

    def gz_copy(way, k, block):
        return remote(
            block, block, gz_send.at[way, k], gz_recv.at[way, k], {"fsdp": at(signs[way], 0)}
        )

    def h0_copy(way, d, block):
        i = d % zs
        return remote(
            block, block, h0_send.at[way, i], h0_recv.at[way, i], {"fsdp": at(0, signs[way])}
        )

    def h1_copy(d, block):
        i = d % zs
        return remote(
            block, block, h1_send.at[i], h1_recv.at[i], {"fsdp": at(0, signs[of_way(d)])}
        )

    def gz_step(s):
        for way in range(2):
            d = -signs[way] * s
            if (s == half and way == 0) or (s == 0 and way == 1):
                continue
            block = second(d, 0)
            if s > 0:
                gz_copy(way, s - 1, block).wait_recv()
            for to in range(2) if s == 0 else (way,):
                if s < half - 1 + to:
                    start(gz_copy(to, s, block))

    def h0_step(s):
        for d in both(s):
            for way in range(2):
                start(h0_copy(way, d, second(d, 0)))

    def both(s):
        return (s,) if s in (0, half) else (s, -s)

    def h1_step(s):
        for d in both(s):
            for way in range(2):
                block = second(d, -signs[way])
                h0_copy(way, d, block).wait_recv()
                if way == of_way(d):
                    start(h1_copy(d, block))

    def h1_end(s):
        for d in both(s):
            h1_copy(d, second(d, 2)).wait_recv()
            project(d, ta, tb)

    def project(dz, low, count):
        head = lax.rem(z + dz + zs, zs) * ys
        total = acc_v[low : low + count]
        for pair in range(ys // 2):
            lhs = jnp.concatenate(
                [ctx_v[head + 2 * pair + i, low : low + count] for i in range(2)], axis=1
            )
            row = pl.multiple_of((head + 2 * pair) * HD, 2 * HD)
            total = total + dot(lhs, w_v[pl.ds(row, 2 * HD), :])
        acc_v[low : low + count] = total

    def ga_slot(s, fresh_from=0):
        if s < half:
            for j in range(fresh_from, ys):
                ga_step(s, j)
        else:
            for j in range(ys):
                way = 0 if mine(0, j) else 1
                ga_copy(way, half - 1, j, first(half, -j)).wait_recv()
        for d in both(s):
            project(d, 0, ta)

    loads[0].wait()
    fresh = fresh_v[...].astype(F32)
    fresh_sq = token_sums(fresh * fresh)
    loads[1].wait()
    held = held_v[...].astype(F32)
    held_sq = token_sums(held * held)
    stats = jnp.concatenate(
        [fresh_sq[:, :HD], fresh_sq[:, HD:], held_sq[:, :HD], held_sq[:, HD:],
         jnp.zeros((4, HD), F32)], axis=0
    )
    loads[2].wait()
    upt_v[...] = jnp.transpose(up_v[...].astype(F32)).astype(BF16)
    pl.semaphore_wait(barrier, len(peers))
    y_sum_start(stats, stat_y, sy_send, sy_recv)
    for load in loads[3:]:
        load.wait()
    gain = gain_v[...]
    farthest = [half]
    for k in range(half - 1, 0, -1):
        farthest += [k, -k]
    farthest.append(0)
    for j in range(ys):
        a_step(0, j)
        start(a_copy(0 if mine(0, j) else 1, 0, j))
    for d in farthest:
        b0_out[d % zs] = partial(d, 2, fa, fb).astype(BF16)
        start(b0_copy(d))

    def stats_middle():
        stat_v[...] = y_sum_end(stat_y, sy_send, sy_recv)
        z_sum_start(stat_v, stat_z, sz_send, sz_recv)

    def mirror_start(i):
        src, dst = ((held_v, fetched_v), (fresh_v, moved_ref))[i]
        start(remote(src, dst, mir_send.at[i], mir_recv.at[i], mirror))

    def forward_attention():
        inverse = lax.rsqrt(z_sum_end(stat_v, stat_z, sz_send, sz_recv) / width + EPSILON)
        stat_m[0] = inverse
        start(remote(stat_m.at[0], stat_m.at[1], mir_send.at[2], mir_recv.at[2], mirror))
        values = fresh_v[...].astype(F32)
        normed = (values * columns(inverse, 0) * gain).astype(BF16)
        weights = causal_probs(normed).astype(BF16)
        ctx_v[me] = dot(weights, normed[:, HD:]).astype(BF16)
        acc_v[...] = values

    def backward_probs():
        remote(held_v, fetched_v, mir_send.at[0], mir_recv.at[0], mirror).wait_recv()
        remote(stat_m.at[0], stat_m.at[1], mir_send.at[2], mir_recv.at[2], mirror).wait_recv()
        normed_v[...] = (fetched_v[...].astype(F32) * columns(stat_m[1], 2) * gain).astype(BF16)
        probs_v[...] = causal_probs(normed_v[...])

    def backward_attention():
        grad_t = own_v[:fa]
        for j in range(ys - 1):
            ay_copy(j).wait_recv()
            grad_t = grad_t + ay_in[j].astype(F32)
        own_v[:fa] = grad_t
        dcontext = jnp.transpose(own_v[...]).astype(BF16)
        probs = probs_v[...]
        queries, keyvals = normed_v[:, :HD], normed_v[:, HD:]
        dprob = dot_t(dcontext, keyvals)
        dvalue = dot(jnp.transpose(probs).astype(BF16), dcontext)
        dscore = probs * (dprob - jnp.sum(dprob * probs, axis=-1, keepdims=True)) * (HD**-0.5)
        dquery = dot(dscore.astype(BF16), keyvals)
        dkey = dot(jnp.transpose(dscore).astype(BF16), queries)
        scaled = jnp.concatenate([dquery, dvalue + dkey], axis=1) * gain
        probs_v[...] = scaled
        moment = token_sums(scaled * fetched_v[...].astype(F32))
        mom_v[...] = jnp.concatenate(
            [moment[:, :HD], moment[:, HD:], jnp.zeros((6, HD), F32)], axis=0
        )
        z_sum_start(mom_v, mom_z, mz_send, mz_recv)

    def moment_middle():
        y_sum_start(z_sum_end(mom_v, mom_z, mz_send, mz_recv), mom_y, my_send, my_recv)

    def backward_end():
        total = columns(y_sum_end(mom_y, my_send, my_recv), 0)
        inverse = columns(stat_m[1], 2)
        grad_in = up_v[...].astype(F32) + inverse * probs_v[...]
        grad_in = grad_in - fetched_v[...].astype(F32) * (inverse**3 * total / width)
        gin_ref[...] = grad_in.astype(BF16)

    def gy_start():
        for d in range(1, ys):
            start(gy_copy(d, first(0, 0)))

    beside = {(k, j): [] for k in range(1, half) for j in range(ys)}

    def add(slot, step, what, *of):
        at_step = (slot, step) if slot < half else (half - 1, ys - 1)
        beside[at_step].append(functools.partial(what, *of))

    for i, d in enumerate(farthest[:3]):
        add(1, i + 1, b1_step, d)
    add(1, 3, stats_middle)
    for i, d in enumerate(farthest[3:7]):
        add(2, i, b1_step, d)
    add(2, 3, mirror_start, 0)
    for d in farthest[7:]:
        add(2, 3, b1_step, d)
    add(3, 0, forward_attention)
    add(3, 0, gz_step, 0)
    add(3, 2, gy_start)
    add(3, 3, ga_step, 0, 0)
    places = ((3, 3), (4, 1), (4, 3), (5, 1), (5, 3))
    for k in range(half - 1):
        add(*places[k], bz_step, k)
        add(*places[k], gz_step, k + 1)
    if half < 3:
        add(3, 3, gz_step, 2)
    for k in range(1, half):
        for j in range(ys):
            a_step(k, j)
            for what in beside[k, j]:
                what()
    for j in range(ys):
        a_last(j)
    h0_step(0)
    bz_step(half - 1)
    if half > 2:
        gz_step(half)
    bz_last()
    backward_probs()
    h0_step(1)
    ga_slot(0, 1)
    backward_attention()
    h0_turn = iter(range(2, half + 1))
    h1_turn = iter(range(half + 1))
    h1_begun = 0
    h1_done = 0
    for s in range(1, half):
        for count in range(2 if s == 2 else 1):
            h0_next = next(h0_turn, None)
            if h0_next is not None:
                h0_step(h0_next)
        ga_slot(s)
        if s == 1:
            mirror_start(1)
        for count in range(2 if s in (1, 3) else 1):
            h1_step(next(h1_turn))
            h1_begun += 1
        while h1_done < h1_begun - 2:
            h1_end(h1_done)
            h1_done += 1
        if s == min(2, half - 1):
            moment_middle()
        if s == min(4, half - 1):
            backward_end()
    for s in h0_turn:
        h0_step(s)
    drain()
    ga_slot(half)
    for s in h1_turn:
        h1_step(s)
    for s in range(h1_done, half + 1):
        h1_end(s)
    out_ref[...] = acc_v[...].astype(BF16)
    remote(fresh_v, moved_ref, mir_send.at[1], mir_recv.at[1], mirror).wait_recv()
    drain()


def local(ys, sections, section_input, stash_held, upstream, norm_gain, out_weight):
    tokens, part = section_input.shape[1:]
    heads = out_weight.shape[1] // HD
    zs = heads // ys
    half = zs // 2
    fb = HD - SUM_FIRST
    dma = pltpu.SemaphoreType.DMA
    square = (tokens, part)
    whole = pl.BlockSpec(memory_space=pltpu.VMEM)
    anywhere = pl.BlockSpec(memory_space=pl.ANY)
    buffers = [
        (square, BF16),
        (square, BF16),
        (square, BF16),
        ((1, part), F32),
        ((heads * HD, part), BF16),
        ((part, tokens), BF16),
        (square, BF16),
        (square, F32),
        ((HD, tokens), F32),
        ((tokens, tokens), F32),
        (square, BF16),
        ((2, half, ys, SUM_FIRST, tokens), BF16),
        ((2, half, ys, SUM_FIRST, tokens), BF16),
        ((ys, SUM_FIRST, tokens), BF16),
        ((ys, SUM_FIRST, tokens), BF16),
        ((zs, fb, tokens), BF16),
        ((zs, fb, tokens), BF16),
        ((2, zs, fb, tokens), BF16),
        ((2, zs, fb, tokens), BF16),
        ((2, half, fb, tokens), BF16),
        ((2, half, fb, tokens), BF16),
        ((heads, tokens, HD), BF16),
        ((8, HD), F32),
        ((zs, 8, HD), F32),
        ((ys, 8, HD), F32),
        ((2, 8, HD), F32),
        ((8, HD), F32),
        ((zs, 8, HD), F32),
        ((ys, 8, HD), F32),
    ]
    semaphores = [
        (8,), (3,), (3,), (2, half, ys), (2, half, ys), (ys,), (ys,),
        (zs,), (zs,), (2, zs), (2, zs), (2, half), (2, half),
        (ys,), (ys,), (2, half, ys), (2, half, ys), (2, half), (2, half),
        (2, zs), (2, zs), (zs,), (zs,),
        (zs,), (zs,), (ys,), (ys,), (zs,), (zs,), (ys,), (ys,),
    ]
    result = jax.ShapeDtypeStruct(square, BF16)
    output, moved, grad_in = pl.pallas_call(
        functools.partial(body, sections, zs, ys),
        out_shape=(result, result, result),
        in_specs=[pl.BlockSpec(memory_space=pltpu.HBM)] * 5,
        out_specs=(whole, anywhere, whole),
        scratch_shapes=[pltpu.VMEM(*b) for b in buffers] + [dma(s) for s in semaphores],
        compiler_params=pltpu.CompilerParams(
            collective_id=0, has_side_effects=True, vmem_limit_bytes=60 * 1024 * 1024
        ),
        name="relay_tick",
    )(section_input[0], stash_held[0], upstream[0], norm_gain, out_weight[0])
    return output[None], moved[None], grad_in[None]


def solution(mesh):
    wide = P("section", None, "fsdp")
    return jax.shard_map(
        functools.partial(local, YS, mesh.shape["section"]),
        mesh=mesh,
        in_specs=(wide, wide, wide, P("section", "fsdp"), wide),
        out_specs=(wide, wide, wide),
        check_vma=False,
    )
```
